256 devices in a mesh: dp: 32 (over y, x, core), mp: 8 (over z).
Axes of the slice: x: 4, y: 4, z: 8, core: 2. Of those that a mesh axis runs over, the one named last changes fastest.
Arguments:
- queries: bfloat16 [65536, 4096], P('dp', 'mp'), may hold values from -5 to 5
- rotated_key_state: bfloat16 [65536, 1024], P('dp', 'mp'), may hold values from -5 to 5
- value_state_rows: bfloat16 [65536, 1024], P('dp', 'mp'), may hold values from -6 to 6
- out_weight: bfloat16 [4096, 8192], P('mp', 'dp'), may hold values from -0.375 to 0.375
- segments: int32 [65536], P('dp'), may hold values from -1 to 4, as said below
- send_plan: int32 [512], replicated, may hold values from -1 to 255, as said below
Outputs:
- projected: bfloat16 [32768, 8192], P(('dp', 'mp'))
The draws below stay inside these ranges and needn't reach their ends.
Inputs may be any that keep to these rules, and one draw needn't show every extreme that they name: `segments`: in each group segment numbers start at 0 on the first row, never fall, and are -1 exactly on the rows of dead blocks, which follow the live ones. No response is longer than 1024 tokens; the first response of each group has 1024 tokens unless the group's live rows end before. Some group has all 16 blocks live and some group none. `send_plan`: live blocks (those with segment numbers of 0 or more) name each balanced slot exactly once, slot s meaning row block s of the balanced order and data group s // 8; dead blocks hold -1. From one group at most 1 block go to the same group, and some pair of groups reaches 1.
All inputs are finite; a program needn't handle non-finite values.
Results may differ from the reference program's by a relative error of at most 0.017.
Values may be sent and summed in bfloat16 or wider, within the bound.
No kernel may reach another device: no remote copies, remote signals or barrier semaphores. Data moves between devices by JAX's collectives and lax.ppermute only.
A program may use at most 128 MiB of HBM per device.

```python
import math
import jax
import jax.numpy as jnp
from jax import lax

D = 8192
QUERY_HEADS = 32
KEY_VALUE_HEADS = 8
HEAD_SIZE = 128
RESPONSE_BLOCK = 128
QUERY_BLOCK = 512
LMAX = 1024
BAL = 8
CAP = 16
GROUP_ROWS = 2048
ROWS_BAL = 1024
TOKEN_SLOTS = 65536
TOK_BAL = 32768
N_DP = 32
N_MP = 8


def block_layout(key):
    groups = TOKEN_SLOTS // GROUP_ROWS
    key_swing = jax.random.fold_in(key, 101)
    key_order = jax.random.fold_in(key, 102)
    key_spread = jax.random.fold_in(key, 103)
    key_length = jax.random.fold_in(key, 104)
    order = jax.random.permutation(key_order, groups)
    swings = jax.random.randint(key_swing, (groups // 2,), 0, BAL + 1)
    swings = swings.at[0].set(BAL)
    counts = jnp.zeros((groups,), jnp.int32)
    counts = counts.at[order[0::2]].set(BAL + swings).at[order[1::2]].set(BAL - swings)
    first_index = jnp.cumsum(counts) - counts
    block_index = jnp.arange(CAP)
    alive = block_index[None, :] < counts[:, None]
    global_index = first_index[:, None] + block_index[None, :]
    spread = jax.random.permutation(key_spread, groups)
    target = spread[global_index % groups] * BAL + global_index // groups
    plan = jnp.where(alive, target, -1).reshape(-1).astype(jnp.int32)
    response_count = GROUP_ROWS // (LMAX // 4) + 1
    lengths = jax.random.randint(key_length, (groups, response_count), LMAX // 4, LMAX + 1)
    lengths = lengths.at[:, 0].set(LMAX)
    full_group = counts == CAP
    later_column = jnp.arange(response_count) > 0
    lengths = jnp.where(full_group[:, None] & later_column[None, :], LMAX // 4, lengths)
    ends = jnp.cumsum(lengths, axis=1)
    position = jnp.arange(GROUP_ROWS)
    numbers = jnp.sum((position[None, :, None] >= ends[:, None, :]).astype(jnp.int32), axis=2)
    numbers = jnp.where(position[None, :] < counts[:, None] * RESPONSE_BLOCK, numbers, -1)
    return (plan, numbers.reshape(-1).astype(jnp.int32))


def draw_segments(key, part):
    plan, numbers = block_layout(key)
    return numbers


def draw_send_plan(key, part):
    plan, numbers = block_layout(key)
    return plan


def draw_rotated_key_state(key, part):
    key = jax.random.fold_in(key, 11)
    return jnp.clip(1.4 * jax.random.normal(key, (TOKEN_SLOTS, KEY_VALUE_HEADS * HEAD_SIZE), jnp.float32), -5.0, 5.0).astype(jnp.bfloat16)


def draw_queries(key, part):
    key = jax.random.fold_in(key, 12)
    return jnp.clip(1.4 * jax.random.normal(key, (TOKEN_SLOTS, QUERY_HEADS * HEAD_SIZE), jnp.float32), -5.0, 5.0).astype(jnp.bfloat16)


def levels(key, dims, split, least, largest):
    loudness, own = 1.0, jax.random.fold_in(key, 6)
    for axis_at, shards_of in split:
        heights = jnp.exp(jax.random.uniform(jax.random.fold_in(own, axis_at), (shards_of,), jnp.float32, least / len(split), largest / len(split)))
        loudness = loudness * jnp.repeat(heights, dims[axis_at] // shards_of).reshape([-1 if axis == axis_at else 1 for axis in range(len(dims))])
    return loudness


def centred(key, shape, scale, reach, cuts=(), kind=jnp.bfloat16):
    result = jax.random.normal(key, shape, jnp.float32) * scale
    if len(cuts) > 0:
        result = levels(key, shape, cuts, -0.22, 0.18) * result
    return jnp.clip(result, min=-reach, max=reach).astype(kind)


def setup_inputs(seed: int = 0) -> dict:
    streams_of = jax.random.split(jax.random.key(seed), 7)
    return {
        "queries": draw_queries(jax.random.fold_in(streams_of[6], 71), 0),
        "rotated_key_state": draw_rotated_key_state(jax.random.fold_in(streams_of[6], 71), 0),
        "value_state_rows": centred(streams_of[2], (TOKEN_SLOTS, KEY_VALUE_HEADS * HEAD_SIZE), 1.0, 6.0, ((0, 32), (1, 8))),
        "out_weight": centred(streams_of[3], (QUERY_HEADS * HEAD_SIZE, D), (QUERY_HEADS * HEAD_SIZE // 16) ** -0.5, 0.375, ((0, 8), (1, 32))),
        "segments": draw_segments(jax.random.fold_in(streams_of[6], 71), 0),
        "send_plan": draw_send_plan(jax.random.fold_in(streams_of[6], 71), 0),
    }


def attend_data_group(queries, rotated_key_state, value_state_rows, segments):
    count_of_rows = queries.shape[0]
    group_width = QUERY_HEADS // KEY_VALUE_HEADS
    position = jnp.arange(count_of_rows)
    head_keys = rotated_key_state.astype(jnp.float32).reshape(count_of_rows, KEY_VALUE_HEADS, HEAD_SIZE)
    head_values = value_state_rows.astype(jnp.float32).reshape(count_of_rows, KEY_VALUE_HEADS, HEAD_SIZE)
    pieces = []
    for query_first_row in range(0, count_of_rows, QUERY_BLOCK):
        query_stop_row = query_first_row + QUERY_BLOCK
        head_queries = queries[query_first_row:query_stop_row].astype(jnp.float32).reshape(QUERY_BLOCK, KEY_VALUE_HEADS, group_width, HEAD_SIZE)
        scores = jnp.einsum('qkgd,nkd->kgqn', head_queries, head_keys[:query_stop_row]) * (1.0 / math.sqrt(HEAD_SIZE))
        allowed = (segments[query_first_row:query_stop_row, None] == segments[None, :query_stop_row]) & (position[None, :query_stop_row] <= position[query_first_row:query_stop_row, None])
        scores = jnp.where(allowed[None, None], scores, -1e+30)
        row_max = lax.optimization_barrier(jnp.max(scores, axis=-1, keepdims=True))
        weights = jnp.exp(scores - row_max)
        row_total = lax.optimization_barrier(jnp.sum(weights, axis=-1))
        rounded = lax.optimization_barrier(weights.astype(jnp.bfloat16)).astype(jnp.float32)
        mixture = jnp.einsum('kgqn,nkd->qkgd', rounded, head_values[:query_stop_row])
        mixture = mixture / jnp.transpose(row_total, (2, 0, 1))[..., None]
        pieces.append(mixture.reshape(QUERY_BLOCK, QUERY_HEADS * HEAD_SIZE).astype(jnp.bfloat16))
    return jnp.concatenate(pieces, axis=0)

def reference(queries, rotated_key_state, value_state_rows, out_weight, segments, send_plan):
    attended_rows = lax.map(lambda element_list: attend_data_group(element_list[0], element_list[1], element_list[2], element_list[3]), (queries.reshape(N_DP, GROUP_ROWS, QUERY_HEADS * HEAD_SIZE), rotated_key_state.reshape(N_DP, GROUP_ROWS, KEY_VALUE_HEADS * HEAD_SIZE), value_state_rows.reshape(N_DP, GROUP_ROWS, KEY_VALUE_HEADS * HEAD_SIZE), segments.reshape(N_DP, GROUP_ROWS)))
    slot_count = N_DP * BAL
    landing = jnp.where(send_plan >= 0, send_plan, slot_count).astype(jnp.int32)
    anchor = jnp.zeros((slot_count,), jnp.int32).at[landing].set(jnp.arange(N_DP * CAP, dtype=jnp.int32), mode='drop')
    blocks = attended_rows.reshape(N_DP * CAP, RESPONSE_BLOCK, QUERY_HEADS * HEAD_SIZE)
    placed = blocks[anchor].reshape(N_DP, ROWS_BAL, QUERY_HEADS * HEAD_SIZE)
    head_width = QUERY_HEADS * HEAD_SIZE // N_MP

    def project_rows(row_block):
        summed = jnp.zeros((row_block.shape[0], D), jnp.float32)
        for head_set in range(N_MP):
            partial_sum = jnp.dot(row_block[:, head_set * head_width:(head_set + 1) * head_width], out_weight[head_set * head_width:(head_set + 1) * head_width], preferred_element_type=jnp.float32)
            partial_sum = lax.optimization_barrier(partial_sum.astype(jnp.bfloat16)).astype(jnp.float32)
            summed = summed + partial_sum
        return summed.astype(jnp.bfloat16)
    projected = lax.map(project_rows, placed)
    return projected.reshape(TOK_BAL, D)
```

```python
import functools
import math

import jax
import jax.numpy as jnp
from jax import lax
from jax.experimental import pallas as pl
from jax.experimental.pallas import tpu as pltpu
from jax.sharding import Mesh
from jax.sharding import PartitionSpec as P

HEAD = 128
TQ = 256
BLOCK = 128
BAL = 8
PIECE = 4
PLANE = ("y", "x", "c")
MB = 1024 * 1024

def attention_kernel(seg_s, q_ref, k_ref, v_ref, seg_ref, o_ref, s_scr, m_scr):
    heads = q_ref.shape[1] // HEAD
    t = pl.program_id(0)
    q0 = t * TQ
    first_seg = seg_s[q0]
    c = math.log2(math.e) / math.sqrt(HEAD)

    @pl.when(first_seg >= 0)
    def _():
        lo = jnp.int32(0)
        for j in range(pl.num_programs(0) - 1):
            lo += jnp.where((j < t) & (seg_s[j * TQ + TQ - 1] < first_seg), 1, 0).astype(jnp.int32)
        seg_q = jnp.concatenate(
            [
                jnp.transpose(jnp.broadcast_to(seg_ref[:, pl.ds(pl.multiple_of(q0 + r, 128), 128)], (128, 128)))
                for r in range(0, TQ, 128)
            ],
            axis=0,
        )
        seg_q = jnp.concatenate([seg_q] * (TQ // 128), axis=1)

        def scores(j, diagonal):
            k0 = pl.multiple_of(j * TQ, TQ)
            keys = k_ref[pl.ds(k0, TQ), :]
            allowed = seg_q == jnp.broadcast_to(seg_ref[:, pl.ds(k0, TQ)], (TQ, TQ))
            if diagonal:
                allowed &= lax.broadcasted_iota(jnp.int32, (TQ, TQ), 1) <= lax.broadcasted_iota(jnp.int32, (TQ, TQ), 0)
            bias = jnp.where(allowed, 0.0, -1e30).astype(jnp.float32)
            for h in range(heads):
                s = lax.dot_general(
                    q_ref[:, h * HEAD : (h + 1) * HEAD], keys, (((1,), (1,)), ((), ())), preferred_element_type=jnp.float32
                )
                s = s + bias
                s_scr[h, j - lo] = s
                part = jnp.maximum(s[:, :HEAD], s[:, HEAD:])
                if diagonal:
                    m_scr[h] = part
                else:
                    m_scr[h] = jnp.maximum(m_scr[h], part)

        scores(t, True)

        @pl.loop(lo, t)
        def _(j):
            scores(j, False)

        for h in range(heads):
            top = jnp.max(m_scr[h], axis=1, keepdims=True) * c

            def step(j, carry):
                total, acc = carry
                w = jnp.exp2(s_scr[h, j - lo] * c - top)
                total = total + (w[:, :HEAD] + w[:, HEAD:])
                acc = acc + jnp.dot(
                    w.astype(jnp.bfloat16), v_ref[pl.ds(pl.multiple_of(j * TQ, TQ), TQ), :], preferred_element_type=jnp.float32
                )
                return total, acc

            zero = jnp.zeros((TQ, HEAD), jnp.float32)
            total, acc = lax.fori_loop(lo, t + 1, step, (zero, zero))
            o_ref[:, h * HEAD : (h + 1) * HEAD] = (acc / jnp.sum(total, axis=1, keepdims=True)).astype(jnp.bfloat16)


def attention(queries, keys, values, segments):
    rows, cols = queries.shape
    heads = cols // HEAD
    return pl.pallas_call(
        attention_kernel,
        out_shape=jax.ShapeDtypeStruct((rows, cols), jnp.bfloat16),
        grid_spec=pltpu.PrefetchScalarGridSpec(
            num_scalar_prefetch=1,
            grid=(rows // TQ,),
            in_specs=[
                pl.BlockSpec((TQ, cols), lambda t, *_: (t, 0)),
                pl.BlockSpec((rows, HEAD), lambda t, *_: (0, 0)),
                pl.BlockSpec((rows, HEAD), lambda t, *_: (0, 0)),
                pl.BlockSpec((1, rows), lambda t, *_: (0, 0)),
            ],
            out_specs=pl.BlockSpec((TQ, cols), lambda t, *_: (t, 0)),
            scratch_shapes=[
                pltpu.VMEM((heads, 1024 // TQ + 1, TQ, TQ), jnp.float32),
                pltpu.VMEM((heads, TQ, HEAD), jnp.float32),
            ],
        ),
        compiler_params=pltpu.CompilerParams(vmem_limit_bytes=40 * MB),
        cost_estimate=pl.CostEstimate(flops=4 * rows * 1024 * cols, bytes_accessed=6 * MB, transcendentals=rows * 640 * heads),
        name="attention",
    )(segments, queries, keys, values, segments.reshape(1, rows))


def project_kernel(n_parts, order_s, *refs):
    parts, w_ref, o_ref, rows_scr, acc = refs[:n_parts], refs[n_parts], refs[n_parts + 1], refs[n_parts + 2], refs[n_parts + 3]
    step = pl.program_id(0)
    steps = pl.num_programs(0)
    own, near, far, half_a, half_b = parts[0:2], parts[2:4], parts[4:6], parts[6:8], parts[8:10]
    for c in range(2):
        for k, part in enumerate((own[c], near[c], far[c])):
            rows_scr[(k * 2 + c) * BLOCK : (k * 2 + c + 1) * BLOCK, :] = part[0]

        @pl.when(step < steps // 2)
        def _():
            rows_scr[(6 + c) * BLOCK : (7 + c) * BLOCK, :] = half_a[c][0]

        @pl.when(step >= steps // 2)
        def _():
            rows_scr[(6 + c) * BLOCK : (7 + c) * BLOCK, :] = half_b[c][0]

    wide = w_ref.shape[3]
    for x in range(w_ref.shape[0]):
        product = jnp.dot(rows_scr[...], w_ref[x, 0], preferred_element_type=jnp.float32)

        @pl.when(step == 0)
        def _():
            acc[:, x * wide : (x + 1) * wide] = product

        @pl.when(step > 0)
        def _():
            acc[:, x * wide : (x + 1) * wide] += product

    @pl.when(step == steps - 1)
    def _():
        top = lax.broadcasted_iota(jnp.int32, (8, acc.shape[1]), 0) < PIECE

        @pl.loop(0, BLOCK // 8)
        def _(d2):
            low, high = [], []
            for pair in range(4):
                at = [pl.multiple_of(order_s[2 * pair + i] * BLOCK + d2 * 8, 8) for i in range(2)]
                even, odd = acc[pl.ds(at[0], 8), :], acc[pl.ds(at[1], 8), :]
                low.append(jnp.where(top, even, pltpu.roll(odd, PIECE, 0)))
                high.append(jnp.where(top, pltpu.roll(even, PIECE, 0), odd))
            o_ref[2 * d2] = jnp.concatenate(low, axis=0).astype(jnp.bfloat16)
            o_ref[2 * d2 + 1] = jnp.concatenate(high, axis=0).astype(jnp.bfloat16)


def project(order, parts, weights):
    sets, rows, depth = parts[0].shape
    n_x, _, _, wide = weights.shape
    half = sets // 2
    specs = [pl.BlockSpec((1, rows, depth), lambda i, *_: (i, 0, 0))] * 6
    specs += [pl.BlockSpec((1, rows, depth), lambda i, *_: (jnp.minimum(i, half - 1), 0, 0))] * 2
    specs += [pl.BlockSpec((1, rows, depth), lambda i, *_: (jnp.maximum(i - half, 0), 0, 0))] * 2
    specs += [pl.BlockSpec((n_x, 1, depth, wide), lambda i, *_: (0, i, 0, 0))]
    groups = rows // PIECE
    return pl.pallas_call(
        functools.partial(project_kernel, len(parts)),
        out_shape=jax.ShapeDtypeStruct((groups, 8 * PIECE, n_x * wide), jnp.bfloat16),
        grid_spec=pltpu.PrefetchScalarGridSpec(
            num_scalar_prefetch=1,
            grid=(sets,),
            in_specs=specs,
            out_specs=pl.BlockSpec((groups, 8 * PIECE, n_x * wide), lambda i, *_: (0, 0, 0)),
            scratch_shapes=[
                pltpu.VMEM((8 * rows, depth), jnp.bfloat16),
                pltpu.VMEM((8 * rows, n_x * wide), jnp.float32),
            ],
        ),
        compiler_params=pltpu.CompilerParams(vmem_limit_bytes=40 * MB),
        cost_estimate=pl.CostEstimate(flops=16 * rows * sets * depth * n_x * wide, bytes_accessed=18 * MB, transcendentals=0),
        name="project",
    )(order, *parts, weights)


def gather_rows_of_slots(mine):
    n_y, half = lax.axis_size("y"), mine.shape[0] // 2
    up = [(i, (i + 1) % n_y) for i in range(n_y)]
    down = [(i, (i - 1) % n_y) for i in range(n_y)]
    other = [(0, 1), (1, 0)]
    from_below = lax.ppermute(mine, "y", up)
    from_above = lax.ppermute(mine, "y", down)
    far_a = lax.ppermute(from_below[:half], "y", up)
    far_b = lax.ppermute(from_above[half:], "y", down)
    parts = []
    for part in (mine, from_below, from_above, far_a, far_b):
        parts += [part, lax.ppermute(part, "c", other)]
    return parts


def on_device(queries, keys, values, out_weight, segments, send_plan):
    n_y, n_x, n_c, n_z = (lax.axis_size(a) for a in ("y", "x", "c", "z"))
    groups = n_y * n_x * n_c
    rows, cols = queries.shape
    blocks = rows // BLOCK
    weights = lax.all_gather(out_weight, ("x", "z")).reshape(n_x, n_z, *out_weight.shape)
    attended = attention(queries, keys, values, segments)
    pieces = attended.reshape(blocks, n_x, n_y, n_c, PIECE, cols).transpose(2, 1, 3, 0, 4, 5)
    arrived = lax.all_to_all(pieces.reshape(groups, blocks * PIECE, cols), PLANE, 0, 0, tiled=True)
    slots = jnp.arange(groups * BAL)
    block_of = jnp.sum(
        jnp.where(send_plan[None, :] == slots[:, None], jnp.arange(groups * blocks)[None, :], 0), axis=1, dtype=jnp.int32
    )
    block_of = block_of.reshape(groups, BAL).T.reshape(-1)
    row_of = (block_of[:, None] * PIECE + jnp.arange(PIECE)[None, :]).reshape(-1)
    live = jnp.take(arrived.reshape(groups * blocks * PIECE, cols), row_of, axis=0, mode="clip")
    mine = lax.all_to_all(live.reshape(n_z, groups * PIECE, cols), "z", 0, 0, tiled=True)
    parts = gather_rows_of_slots(mine)
    my_y, my_c = lax.axis_index("y"), lax.axis_index("c")
    place = jnp.array([0, 2, 6, 4], jnp.int32)
    wanted = jnp.arange(n_y * n_c)
    order = place[(my_y - wanted // n_c) % n_y] + (my_c != wanted % n_c)
    projected = project(order.astype(jnp.int32), parts, weights)
    home = lax.all_to_all(projected, PLANE, 0, 0, tiled=True)
    home = home.reshape(n_y, n_x, n_c, n_y * n_c * PIECE, n_x, -1).transpose(1, 3, 0, 4, 2, 5)
    return home.reshape(BLOCK, -1)


def solution(mesh):
    fine = Mesh(mesh.devices.reshape(4, 4, 2, 8), ("y", "x", "c", "z"))
    in_specs = (P(PLANE, "z"), P(PLANE, "z"), P(PLANE, "z"), P("z", PLANE), P(PLANE), P())
    return jax.shard_map(on_device, mesh=fine, in_specs=in_specs, out_specs=P((*PLANE, "z"), None), check_vma=False)
```

```python
import functools
import math

import jax
import jax.numpy as jnp
from jax import lax
from jax.experimental import pallas as pl
from jax.experimental.pallas import tpu as pltpu
from jax.sharding import Mesh
from jax.sharding import PartitionSpec as P

HEAD = 128
TQ = 512
LONGEST = 1024
BLOCK = 128
BAL = 8
PIECE = 4
PLANE = ("y", "x", "c")
MB = 1024 * 1024


def swap_halves(even, odd, axis):
    top = lax.broadcasted_iota(jnp.int32, even.shape, axis) < PIECE
    return jnp.where(top, even, pltpu.roll(odd, PIECE, axis)), jnp.where(top, pltpu.roll(even, PIECE, axis), odd)


def attention_kernel(seg_s, q_ref, k_ref, v_ref, seg_ref, o_ref, bias_scr):
    heads = q_ref.shape[1] // HEAD
    t = pl.program_id(0)
    q0 = t * TQ
    first = seg_s[q0]
    scale = math.log2(math.e) / math.sqrt(HEAD)

    def attend(n):
        k0 = pl.multiple_of((t + 1 - n) * TQ, TQ)
        keys = k_ref[pl.ds(k0, n * TQ), :]
        values = v_ref[pl.ds(k0, n * TQ), :]
        seg_q = jnp.concatenate(
            [
                jnp.transpose(jnp.broadcast_to(seg_ref[:, pl.ds(pl.multiple_of(q0 + r, 128), 128)], (128, 128)))
                for r in range(0, TQ, 128)
            ],
            axis=0,
        )
        seg_q = jnp.concatenate([seg_q] * (TQ // 128), axis=1)
        for j in range(n):
            seg_k = seg_ref[:, pl.ds(pl.multiple_of(k0 + j * TQ, TQ), TQ)]
            allowed = seg_q == jnp.broadcast_to(seg_k, (TQ, TQ))
            if j == n - 1:
                allowed &= lax.broadcasted_iota(jnp.int32, (TQ, TQ), 1) <= lax.broadcasted_iota(jnp.int32, (TQ, TQ), 0)
            bias_scr[:, j * TQ : (j + 1) * TQ] = jnp.where(allowed, 0.0, -1e30).astype(jnp.float32)
        for h in range(heads):
            cols = slice(h * HEAD, (h + 1) * HEAD)
            scores = lax.dot_general(q_ref[:, cols], keys, (((1,), (1,)), ((), ())), preferred_element_type=jnp.float32)
            scores = scores + bias_scr[:, : n * TQ]
            top = jnp.max(scores, axis=1, keepdims=True) * scale
            weights = jnp.exp2(scores * scale - top)
            total = jnp.sum(weights, axis=1, keepdims=True)
            mixed = jnp.dot(weights.astype(jnp.bfloat16), values, preferred_element_type=jnp.float32) / total
            mixed = mixed.reshape(TQ // BLOCK, BLOCK // 8, 8, HEAD)
            runs = []
            for b in range(0, TQ // BLOCK, 2):
                low, high = swap_halves(mixed[b], mixed[b + 1], 1)
                sides = jnp.stack([low, high], axis=1).reshape(4, 4, 2, 8, HEAD)
                runs.append(sides.swapaxes(0, 1).reshape(BLOCK // PIECE, 8, HEAD))
            o_ref[:, :, cols] = jnp.concatenate(runs, axis=1).astype(jnp.bfloat16)

    @pl.when(first >= 0)
    def _():
        tiles = jnp.int32(1)
        for j in range(pl.num_programs(0) - 1):
            tiles += jnp.where((j < t) & (seg_s[j * TQ + TQ - 1] >= first), 1, 0).astype(jnp.int32)
        for n in range(1, LONGEST // TQ + 2):

            @pl.when(tiles == n)
            def _():
                attend(n)


def attention(queries, keys, values, segments):
    rows, cols = queries.shape
    heads = cols // HEAD
    groups = BLOCK // PIECE
    return pl.pallas_call(
        attention_kernel,
        out_shape=jax.ShapeDtypeStruct((groups, rows // groups, cols), jnp.bfloat16),
        grid_spec=pltpu.PrefetchScalarGridSpec(
            num_scalar_prefetch=1,
            grid=(rows // TQ,),
            in_specs=[
                pl.BlockSpec((TQ, cols), lambda t, *_: (t, 0)),
                pl.BlockSpec((rows, HEAD), lambda t, *_: (0, 0)),
                pl.BlockSpec((rows, HEAD), lambda t, *_: (0, 0)),
                pl.BlockSpec((1, rows), lambda t, *_: (0, 0)),
            ],
            out_specs=pl.BlockSpec((groups, TQ // groups, cols), lambda t, *_: (0, t, 0)),
            scratch_shapes=[pltpu.VMEM((TQ, LONGEST + TQ), jnp.float32)],
        ),
        compiler_params=pltpu.CompilerParams(vmem_limit_bytes=58 * MB),
        cost_estimate=pl.CostEstimate(flops=4 * rows * LONGEST * cols, bytes_accessed=6 * MB, transcendentals=rows * 640 * heads),
        name="attention",
    )(segments, queries, keys, values, segments.reshape(1, rows))


def project_kernel(order_s, *refs):
    parts, weights, o_ref = refs[:8], refs[8:12], refs[12]
    rows_scr, w_scr, product, row_sems, w_sems = refs[13:]
    sets, depth = w_scr.shape[1], w_scr.shape[2]
    step = pl.program_id(0)

    def row_copy(k, z):
        into = rows_scr.at[pl.ds(k * BLOCK, BLOCK), pl.ds(z * depth, depth)]
        return pltpu.make_async_copy(parts[k].at[z], into, row_sems.at[k * sets + z])

    def weight_copy(k):
        return pltpu.make_async_copy(weights[k], w_scr.at[k], w_sems.at[k])

    @pl.when(step == 0)
    def _():
        weight_copy(0).start()
        for z in range(sets):
            for k in range(len(parts)):
                row_copy(k, z).start()
        for k in range(1, len(weights)):
            weight_copy(k).start()
        for z in range(sets):
            for k in range(len(parts)):
                row_copy(k, z).wait()

    for k in range(len(weights)):

        @pl.when(step == k)
        def _():
            weight_copy(k).wait()

    w = w_scr[step].reshape(sets * depth, w_scr.shape[3])
    product[...] = jnp.dot(rows_scr[...], w, preferred_element_type=jnp.float32)
    for d2 in range(BLOCK // 8):
        low, high = [], []
        for pair in range(4):
            at = [pl.multiple_of(order_s[2 * pair + i] * BLOCK + d2 * 8, 8) for i in range(2)]
            both = swap_halves(product[pl.ds(at[0], 8), :], product[pl.ds(at[1], 8), :], 0)
            low.append(both[0])
            high.append(both[1])
        o_ref[2 * d2] = jnp.concatenate(low, axis=0).astype(jnp.bfloat16)
        o_ref[2 * d2 + 1] = jnp.concatenate(high, axis=0).astype(jnp.bfloat16)


def project(order, parts, weights):
    sets, rows, depth = parts[0].shape
    wide = weights[0].shape[2]
    n_x = 4
    groups = rows // PIECE
    return pl.pallas_call(
        project_kernel,
        out_shape=jax.ShapeDtypeStruct((groups, 8 * PIECE, n_x * wide), jnp.bfloat16),
        grid_spec=pltpu.PrefetchScalarGridSpec(
            num_scalar_prefetch=1,
            grid=(n_x,),
            in_specs=[pl.BlockSpec(memory_space=pl.ANY)] * 12,
            out_specs=pl.BlockSpec((groups, 8 * PIECE, wide), lambda k, order_s: (0, 0, order_s[8 + k])),
            scratch_shapes=[
                pltpu.VMEM((8 * rows, sets * depth), jnp.bfloat16),
                pltpu.VMEM((n_x, sets, depth, wide), jnp.bfloat16),
                pltpu.VMEM((8 * rows, wide), jnp.float32),
                pltpu.SemaphoreType.DMA((8 * sets,)),
                pltpu.SemaphoreType.DMA((n_x,)),
            ],
        ),
        compiler_params=pltpu.CompilerParams(vmem_limit_bytes=56 * MB),
        cost_estimate=pl.CostEstimate(flops=16 * rows * sets * depth * n_x * wide, bytes_accessed=18 * MB, transcendentals=0),
        name="project",
    )(order, *parts, *weights)


def arrange_kernel(i_ref, o_ref):
    n_y, _, n_c, rows, cols = i_ref.shape
    n_x = pl.num_programs(0)
    wide = cols // n_x
    for y in range(n_y):
        for x in range(n_x):
            for c in range(n_c):
                at = ((y * n_x + x) * n_c + c) * wide
                o_ref[:, at : at + wide] = i_ref[y, 0, c, :, x * wide : (x + 1) * wide]


def arrange(home):
    n_y, n_x, n_c = 4, 4, 2
    _, rows, cols = home.shape
    return pl.pallas_call(
        arrange_kernel,
        out_shape=jax.ShapeDtypeStruct((n_x * rows, n_y * n_c * cols), jnp.bfloat16),
        grid=(n_x,),
        in_specs=[pl.BlockSpec((n_y, 1, n_c, rows, cols), lambda x: (0, x, 0, 0, 0))],
        out_specs=pl.BlockSpec((rows, n_y * n_c * cols), lambda x: (x, 0)),
        compiler_params=pltpu.CompilerParams(vmem_limit_bytes=56 * MB),
        cost_estimate=pl.CostEstimate(flops=0, bytes_accessed=4 * MB, transcendentals=0),
        name="arrange",
    )(home.reshape(n_y, n_x, n_c, rows, cols))


def neighbours(axis, n, apart):
    return [(i, (i + apart) % n) for i in range(n)]


def hop(mine, turn):
    n_y, n_c = lax.axis_size("y"), lax.axis_size("c")
    pairs = [(y * n_c + c, (y + turn * (1 - 2 * c)) % n_y * n_c + c) for y in range(n_y) for c in range(n_c)]
    return lax.ppermute(mine, ("y", "c"), pairs)


def on_device(queries, keys, values, out_weight, segments, send_plan):
    n_y, n_x, n_c, n_z = (lax.axis_size(a) for a in ("y", "x", "c", "z"))
    groups = n_y * n_x * n_c
    rows, cols = queries.shape
    blocks = rows // BLOCK
    w_across = lax.all_gather(lax.ppermute(out_weight, "x", neighbours("x", n_x, 2)), "z")
    w_own = lax.all_gather(out_weight, "z")
    pieces = attention(queries, keys, values, segments)
    arrived = lax.all_to_all(pieces, PLANE, 0, 0, tiled=True)
    w_own, arrived = lax.optimization_barrier((w_own, arrived))
    w_below, w_above = (lax.ppermute(w_own, "x", neighbours("x", n_x, turn)) for turn in (1, -1))
    slots = jnp.arange(groups * BAL)
    block_of = jnp.sum(
        jnp.where(send_plan[None, :] == slots[:, None], jnp.arange(groups * blocks)[None, :], 0), axis=1, dtype=jnp.int32
    )
    block_of = block_of.reshape(groups, BAL).T.reshape(-1)
    row_of = (block_of[:, None] * PIECE + jnp.arange(PIECE)[None, :]).reshape(-1)
    live = jnp.take(arrived.reshape(groups * blocks * PIECE, cols), row_of, axis=0, mode="clip")
    mine = lax.all_to_all(live.reshape(n_z, groups * PIECE, cols), "z", 0, 0, tiled=True)
    ahead, behind = hop(mine, 1), hop(mine, -1)
    parts = []
    for part in (mine, ahead, behind, hop(ahead, 1)):
        parts += [part, lax.ppermute(part, "c", [(0, 1), (1, 0)])]
    my_y, my_x, my_c = (lax.axis_index(a) for a in PLANE)
    from_y, from_c = jnp.divmod(jnp.arange(n_y * n_c), n_c)
    place = jnp.array([[0, 2, 6, 4], [0, 4, 6, 2]], jnp.int32)
    order = place[from_c, (my_y - from_y) % n_y] + (my_c != from_c)
    order = jnp.concatenate([order, (my_x + jnp.array([0, 3, 1, 2], jnp.int32)) % n_x])
    projected = project(order.astype(jnp.int32), parts, (w_own, w_below, w_above, w_across))
    return arrange(lax.all_to_all(projected, PLANE, 0, 0, tiled=True))


def solution(mesh):
    fine = Mesh(mesh.devices.reshape(4, 4, 2, 8), ("y", "x", "c", "z"))
    in_specs = (P(PLANE, "z"), P(PLANE, "z"), P(PLANE, "z"), P("z", PLANE), P(PLANE), P())
    return jax.shard_map(on_device, mesh=fine, in_specs=in_specs, out_specs=P((*PLANE, "z"), None), check_vma=False)
```

```python
import functools
import math

import jax
import jax.numpy as jnp
from jax import lax
from jax.experimental import pallas as pl
from jax.experimental.pallas import tpu as pltpu
from jax.sharding import Mesh
from jax.sharding import PartitionSpec as P

HEAD = 128
TQ = 512
LONGEST = 1024
BLOCK = 128
BAL = 8
PIECE = 4
PLANE = ("y", "x", "c")
MB = 1024 * 1024


def swap_halves(even, odd, axis):
    top = lax.broadcasted_iota(jnp.int32, even.shape, axis) < PIECE
    return jnp.where(top, even, pltpu.roll(odd, PIECE, axis)), jnp.where(top, pltpu.roll(even, PIECE, axis), odd)


def attention_kernel(seg_s, q_ref, k_ref, v_ref, seg_ref, o_ref, bias_scr):
    heads = q_ref.shape[1] // HEAD
    t = pl.program_id(0)
    q0 = t * TQ
    first = seg_s[q0]
    scale = math.log2(math.e) / math.sqrt(HEAD)

    def attend(n):
        k0 = pl.multiple_of((t + 1 - n) * TQ, TQ)
        keys = k_ref[pl.ds(k0, n * TQ), :]
        values = v_ref[pl.ds(k0, n * TQ), :]
        seg_q = jnp.concatenate(
            [
                jnp.transpose(jnp.broadcast_to(seg_ref[:, pl.ds(pl.multiple_of(q0 + r, 128), 128)], (128, 128)))
                for r in range(0, TQ, 128)
            ],
            axis=0,
        )
        seg_q = jnp.concatenate([seg_q] * (TQ // 128), axis=1)
        for j in range(n):
            seg_k = seg_ref[:, pl.ds(pl.multiple_of(k0 + j * TQ, TQ), TQ)]
            allowed = seg_q == jnp.broadcast_to(seg_k, (TQ, TQ))
            if j == n - 1:
                allowed &= lax.broadcasted_iota(jnp.int32, (TQ, TQ), 1) <= lax.broadcasted_iota(jnp.int32, (TQ, TQ), 0)
            bias_scr[:, j * TQ : (j + 1) * TQ] = jnp.where(allowed, 0.0, -1e30).astype(jnp.float32)
        for h in range(heads):
            cols = slice(h * HEAD, (h + 1) * HEAD)
            scores = lax.dot_general(q_ref[:, cols], keys, (((1,), (1,)), ((), ())), preferred_element_type=jnp.float32)
            scores = scores + bias_scr[:, : n * TQ]
            top = jnp.max(scores, axis=1, keepdims=True) * scale
            weights = jnp.exp2(scores * scale - top)
            total = jnp.sum(weights, axis=1, keepdims=True)
            mixed = jnp.dot(weights.astype(jnp.bfloat16), values, preferred_element_type=jnp.float32) / total
            mixed = mixed.reshape(TQ // BLOCK, BLOCK // 8, 8, HEAD)
            runs = []
            for b in range(0, TQ // BLOCK, 2):
                low, high = swap_halves(mixed[b], mixed[b + 1], 1)
                sides = jnp.stack([low, high], axis=1).reshape(4, 4, 2, 8, HEAD)
                runs.append(sides.swapaxes(0, 1).reshape(BLOCK // PIECE, 8, HEAD))
            o_ref[:, :, cols] = jnp.concatenate(runs, axis=1).astype(jnp.bfloat16)

    @pl.when(first >= 0)
    def _():
        tiles = jnp.int32(1)
        for j in range(pl.num_programs(0) - 1):
            tiles += jnp.where((j < t) & (seg_s[j * TQ + TQ - 1] >= first), 1, 0).astype(jnp.int32)
        for n in range(1, LONGEST // TQ + 2):

            @pl.when(tiles == n)
            def _():
                attend(n)


def attention(queries, keys, values, segments):
    rows, cols = queries.shape
    heads = cols // HEAD
    groups = BLOCK // PIECE
    return pl.pallas_call(
        attention_kernel,
        out_shape=jax.ShapeDtypeStruct((groups, rows // groups, cols), jnp.bfloat16),
        grid_spec=pltpu.PrefetchScalarGridSpec(
            num_scalar_prefetch=1,
            grid=(rows // TQ,),
            in_specs=[
                pl.BlockSpec((TQ, cols), lambda t, *_: (t, 0)),
                pl.BlockSpec((rows, HEAD), lambda t, *_: (0, 0)),
                pl.BlockSpec((rows, HEAD), lambda t, *_: (0, 0)),
                pl.BlockSpec((1, rows), lambda t, *_: (0, 0)),
            ],
            out_specs=pl.BlockSpec((groups, TQ // groups, cols), lambda t, *_: (0, t, 0)),
            scratch_shapes=[pltpu.VMEM((TQ, LONGEST + TQ), jnp.float32)],
        ),
        compiler_params=pltpu.CompilerParams(vmem_limit_bytes=58 * MB),
        cost_estimate=pl.CostEstimate(flops=4 * rows * LONGEST * cols, bytes_accessed=6 * MB, transcendentals=rows * 640 * heads),
        name="attention",
    )(segments, queries, keys, values, segments.reshape(1, rows))


def project_kernel(order_s, *refs):
    parts, weights, o_ref = refs[:8], refs[8:12], refs[12]
    rows_scr, w_scr, product, row_sems, w_sems = refs[13:]
    sets, depth = w_scr.shape[1], w_scr.shape[2]
    step = pl.program_id(0)

    def row_copy(k, z):
        into = rows_scr.at[pl.ds(k * BLOCK, BLOCK), pl.ds(z * depth, depth)]
        source = parts[k].at[lax.rem(order_s[12] + sets - z, sets)]
        return pltpu.make_async_copy(source, into, row_sems.at[k * sets + z])

    def weight_copy(k):
        return pltpu.make_async_copy(weights[k], w_scr.at[k], w_sems.at[k])

    @pl.when(step == 0)
    def _():
        weight_copy(0).start()
        for z in range(sets):
            for k in range(len(parts)):
                row_copy(k, z).start()
        for k in range(1, len(weights)):
            weight_copy(k).start()
        for z in range(sets):
            for k in range(len(parts)):
                row_copy(k, z).wait()

    for k in range(len(weights)):

        @pl.when(step == k)
        def _():
            weight_copy(k).wait()

    w = w_scr[step].reshape(sets * depth, w_scr.shape[3])
    product[...] = jnp.dot(rows_scr[...], w, preferred_element_type=jnp.float32)
    for d2 in range(BLOCK // 8):
        low, high = [], []
        for pair in range(4):
            at = [pl.multiple_of(order_s[2 * pair + i] * BLOCK + d2 * 8, 8) for i in range(2)]
            both = swap_halves(product[pl.ds(at[0], 8), :], product[pl.ds(at[1], 8), :], 0)
            low.append(both[0])
            high.append(both[1])
        o_ref[2 * d2] = jnp.concatenate(low, axis=0).astype(jnp.bfloat16)
        o_ref[2 * d2 + 1] = jnp.concatenate(high, axis=0).astype(jnp.bfloat16)


def project(order, parts, weights):
    sets, rows, depth = parts[0].shape
    wide = weights[0].shape[2]
    n_x = 4
    groups = rows // PIECE
    return pl.pallas_call(
        project_kernel,
        out_shape=jax.ShapeDtypeStruct((groups, 8 * PIECE, n_x * wide), jnp.bfloat16),
        grid_spec=pltpu.PrefetchScalarGridSpec(
            num_scalar_prefetch=1,
            grid=(n_x,),
            in_specs=[pl.BlockSpec(memory_space=pl.ANY)] * 12,
            out_specs=pl.BlockSpec((groups, 8 * PIECE, wide), lambda k, order_s: (0, 0, order_s[8 + k])),
            scratch_shapes=[
                pltpu.VMEM((8 * rows, sets * depth), jnp.bfloat16),
                pltpu.VMEM((n_x, sets, depth, wide), jnp.bfloat16),
                pltpu.VMEM((8 * rows, wide), jnp.float32),
                pltpu.SemaphoreType.DMA((8 * sets,)),
                pltpu.SemaphoreType.DMA((n_x,)),
            ],
        ),
        compiler_params=pltpu.CompilerParams(vmem_limit_bytes=56 * MB),
        cost_estimate=pl.CostEstimate(flops=16 * rows * sets * depth * n_x * wide, bytes_accessed=18 * MB, transcendentals=0),
        name="project",
    )(order, *parts, *weights)


def arrange_kernel(i_ref, o_ref):
    n_y, _, n_c, rows, cols = i_ref.shape
    n_x = pl.num_programs(0)
    wide = cols // n_x
    for y in range(n_y):
        for x in range(n_x):
            for c in range(n_c):
                at = ((y * n_x + x) * n_c + c) * wide
                o_ref[:, at : at + wide] = i_ref[y, 0, c, :, x * wide : (x + 1) * wide]


def arrange(home):
    n_y, n_x, n_c = 4, 4, 2
    _, rows, cols = home.shape
    return pl.pallas_call(
        arrange_kernel,
        out_shape=jax.ShapeDtypeStruct((n_x * rows, n_y * n_c * cols), jnp.bfloat16),
        grid=(n_x,),
        in_specs=[pl.BlockSpec((n_y, 1, n_c, rows, cols), lambda x: (0, x, 0, 0, 0))],
        out_specs=pl.BlockSpec((rows, n_y * n_c * cols), lambda x: (x, 0)),
        compiler_params=pltpu.CompilerParams(vmem_limit_bytes=56 * MB),
        cost_estimate=pl.CostEstimate(flops=0, bytes_accessed=4 * MB, transcendentals=0),
        name="arrange",
    )(home.reshape(n_y, n_x, n_c, rows, cols))


def neighbours(axis, n, apart):
    return [(i, (i + apart) % n) for i in range(n)]


def join_kernel(*refs):
    *sources, o_ref, held, in_sems, out_sems = refs
    fetch = [pltpu.make_async_copy(source, held.at[k], in_sems.at[k]) for k, source in enumerate(sources)]
    store = [pltpu.make_async_copy(held.at[k], o_ref.at[k], out_sems.at[k]) for k in range(len(sources))]
    for copy in fetch:
        copy.start()
    for arriving, leaving in zip(fetch, store):
        arriving.wait()
        leaving.start()
    for copy in store:
        copy.wait()


def join(shards):
    n = len(shards)
    return pl.pallas_call(
        join_kernel,
        out_shape=jax.ShapeDtypeStruct((n, *shards[0].shape), shards[0].dtype),
        in_specs=[pl.BlockSpec(memory_space=pl.ANY)] * n,
        out_specs=pl.BlockSpec(memory_space=pl.ANY),
        scratch_shapes=[
            pltpu.VMEM((n, *shards[0].shape), shards[0].dtype),
            pltpu.SemaphoreType.DMA((n,)),
            pltpu.SemaphoreType.DMA((n,)),
        ],
        compiler_params=pltpu.CompilerParams(vmem_limit_bytes=56 * MB),
        cost_estimate=pl.CostEstimate(flops=0, bytes_accessed=4 * MB, transcendentals=0),
        name="join",
    )(*shards)


def ring(shard, before, after, axis):
    n = lax.axis_size(axis)
    before, after = [shard, before], [after]
    for _ in range(n // 2 - 1):
        before.append(lax.ppermute(before[-1], axis, neighbours(axis, n, 1)))
    for _ in range(n - n // 2 - 2):
        after.append(lax.ppermute(after[-1], axis, neighbours(axis, n, -1)))
    return before + after[::-1]


def hop(mine, axis, turn):
    n, n_c = lax.axis_size(axis), lax.axis_size("c")
    pairs = [(i * n_c + c, (i + turn * (1 - 2 * c)) % n * n_c + c) for i in range(n) for c in range(n_c)]
    return lax.ppermute(mine, (axis, "c"), pairs)


def on_device(queries, keys, values, out_weight, segments, send_plan):
    n_y, n_x, n_c, n_z = (lax.axis_size(a) for a in ("y", "x", "c", "z"))
    my_y, my_x, my_c = (lax.axis_index(a) for a in PLANE)
    groups = n_y * n_x * n_c
    rows, cols = queries.shape
    blocks = rows // BLOCK
    z_before, z_after = (lax.ppermute(out_weight, "z", neighbours("z", n_z, turn)) for turn in (1, -1))
    pieces = attention(queries, keys, values, segments)
    z_before, z_after, pieces = lax.optimization_barrier((z_before, z_after, pieces))
    arrived = lax.all_to_all(pieces, PLANE, 0, 0, tiled=True)
    shards, arrived = lax.optimization_barrier((ring(out_weight, z_before, z_after, "z"), arrived))
    w_own = join(shards)
    w_ahead, w_behind = hop(w_own, "x", 1), hop(w_own, "x", -1)
    slots = jnp.arange(groups * BAL)
    block_of = jnp.sum(
        jnp.where(send_plan[None, :] == slots[:, None], jnp.arange(groups * blocks)[None, :], 0), axis=1, dtype=jnp.int32
    )
    block_of = block_of.reshape(groups, BAL).T.reshape(-1)
    row_of = (block_of[:, None] * PIECE + jnp.arange(PIECE)[None, :]).reshape(-1)
    live = jnp.take(arrived.reshape(groups * blocks * PIECE, cols), row_of, axis=0, mode="clip")
    mine = lax.all_to_all(live.reshape(n_z, groups * PIECE, cols), "z", 0, 0, tiled=True)
    ahead = hop(mine, "y", 1)
    w_ahead, ahead, mine = lax.optimization_barrier((w_ahead, ahead, mine))
    w_across, behind = hop(w_ahead, "x", 1), hop(mine, "y", -1)
    parts = []
    for part in (mine, ahead, behind, hop(ahead, "y", 1)):
        parts += [part, lax.ppermute(part, "c", [(0, 1), (1, 0)])]
    from_y, from_c = jnp.divmod(jnp.arange(n_y * n_c), n_c)
    place = jnp.array([[0, 2, 6, 4], [0, 4, 6, 2]], jnp.int32)
    order = place[from_c, (my_y - from_y) % n_y] + (my_c != from_c)
    turn = 1 - 2 * my_c
    from_x = (my_x - turn * jnp.array([0, 1, -1, 2])) % n_x
    order = jnp.concatenate([order, from_x, lax.axis_index("z").reshape(1)])
    projected = project(order.astype(jnp.int32), parts, (w_own, w_ahead, w_behind, w_across))
    return arrange(lax.all_to_all(projected, PLANE, 0, 0, tiled=True))


def solution(mesh):
    fine = Mesh(mesh.devices.reshape(4, 4, 2, 8), ("y", "x", "c", "z"))
    in_specs = (P(PLANE, "z"), P(PLANE, "z"), P(PLANE, "z"), P("z", PLANE), P(PLANE), P())
    return jax.shard_map(on_device, mesh=fine, in_specs=in_specs, out_specs=P((*PLANE, "z"), None), check_vma=False)
```

```python
import functools
import math

import jax
import jax.numpy as jnp
from jax import lax
from jax.experimental import pallas as pl
from jax.experimental.pallas import tpu as pltpu
from jax.sharding import Mesh
from jax.sharding import PartitionSpec as P

HEAD = 128
TQ = 512
LONGEST = 1024
BLOCK = 128
BAL = 8
PIECE = 4
PLANE = ("y", "x", "c")
MB = 1024 * 1024


def swap_halves(even, odd, axis):
    top = lax.broadcasted_iota(jnp.int32, even.shape, axis) < PIECE
    return jnp.where(top, even, pltpu.roll(odd, PIECE, axis)), jnp.where(top, pltpu.roll(even, PIECE, axis), odd)


def attention_kernel(seg_s, q_ref, k_ref, v_ref, seg_ref, o_ref, bias_scr):
    heads = q_ref.shape[1] // HEAD
    t = pl.program_id(0)
    q0 = t * TQ
    first = seg_s[q0]
    scale = math.log2(math.e) / math.sqrt(HEAD)

    def attend(n):
        k0 = pl.multiple_of((t + 1 - n) * TQ, TQ)
        keys = k_ref[pl.ds(k0, n * TQ), :]
        values = v_ref[pl.ds(k0, n * TQ), :]
        seg_q = jnp.concatenate(
            [
                jnp.transpose(jnp.broadcast_to(seg_ref[:, pl.ds(pl.multiple_of(q0 + r, 128), 128)], (128, 128)))
                for r in range(0, TQ, 128)
            ],
            axis=0,
        )
        seg_q = jnp.concatenate([seg_q] * (TQ // 128), axis=1)
        for j in range(n):
            seg_k = seg_ref[:, pl.ds(pl.multiple_of(k0 + j * TQ, TQ), TQ)]
            allowed = seg_q == jnp.broadcast_to(seg_k, (TQ, TQ))
            if j == n - 1:
                allowed &= lax.broadcasted_iota(jnp.int32, (TQ, TQ), 1) <= lax.broadcasted_iota(jnp.int32, (TQ, TQ), 0)
            bias_scr[:, j * TQ : (j + 1) * TQ] = jnp.where(allowed, 0.0, -1e30).astype(jnp.float32)
        for h in range(heads):
            cols = slice(h * HEAD, (h + 1) * HEAD)
            scores = lax.dot_general(q_ref[:, cols], keys, (((1,), (1,)), ((), ())), preferred_element_type=jnp.float32)
            scores = scores + bias_scr[:, : n * TQ]
            top = jnp.max(scores, axis=1, keepdims=True) * scale
            weights = jnp.exp2(scores * scale - top)
            total = jnp.sum(weights, axis=1, keepdims=True)
            mixed = jnp.dot(weights.astype(jnp.bfloat16), values, preferred_element_type=jnp.float32) / total
            mixed = mixed.reshape(TQ // BLOCK, BLOCK // 8, 8, HEAD)
            runs = []
            for b in range(0, TQ // BLOCK, 2):
                low, high = swap_halves(mixed[b], mixed[b + 1], 1)
                sides = jnp.stack([low, high], axis=1).reshape(4, 4, 2, 8, HEAD)
                runs.append(sides.swapaxes(0, 1).reshape(BLOCK // PIECE, 8, HEAD))
            o_ref[:, :, cols] = jnp.concatenate(runs, axis=1).astype(jnp.bfloat16)

    @pl.when(first < 0)
    def _():
        o_ref[...] = jnp.zeros_like(o_ref)

    @pl.when(first >= 0)
    def _():
        tiles = jnp.int32(1)
        for j in range(pl.num_programs(0) - 1):
            tiles += jnp.where((j < t) & (seg_s[j * TQ + TQ - 1] >= first), 1, 0).astype(jnp.int32)
        for n in range(1, LONGEST // TQ + 2):

            @pl.when(tiles == n)
            def _():
                attend(n)


def attention(queries, keys, values, segments):
    rows, cols = queries.shape
    heads = cols // HEAD
    groups = BLOCK // PIECE
    return pl.pallas_call(
        attention_kernel,
        out_shape=jax.ShapeDtypeStruct((groups, rows // groups, cols), jnp.bfloat16),
        grid_spec=pltpu.PrefetchScalarGridSpec(
            num_scalar_prefetch=1,
            grid=(rows // TQ,),
            in_specs=[
                pl.BlockSpec((TQ, cols), lambda t, *_: (t, 0)),
                pl.BlockSpec((rows, HEAD), lambda t, *_: (0, 0)),
                pl.BlockSpec((rows, HEAD), lambda t, *_: (0, 0)),
                pl.BlockSpec((1, rows), lambda t, *_: (0, 0)),
            ],
            out_specs=pl.BlockSpec((groups, TQ // groups, cols), lambda t, *_: (0, t, 0)),
            scratch_shapes=[pltpu.VMEM((TQ, LONGEST + TQ), jnp.float32)],
        ),
        compiler_params=pltpu.CompilerParams(vmem_limit_bytes=58 * MB),
        cost_estimate=pl.CostEstimate(flops=4 * rows * LONGEST * cols, bytes_accessed=6 * MB, transcendentals=rows * 640 * heads),
        name="attention",
    )(segments, queries, keys, values, segments.reshape(1, rows))


def project_kernel(order_s, *refs):
    parts, weights, o_ref = refs[:8], refs[8:12], refs[12]
    rows_scr, w_scr, product, row_sems, w_sems = refs[13:]
    sets, depth = w_scr.shape[1], w_scr.shape[2]
    step = pl.program_id(0)

    def row_copy(k, z):
        into = rows_scr.at[pl.ds(k * BLOCK, BLOCK), pl.ds(z * depth, depth)]
        source = parts[k].at[lax.rem(order_s[12] + sets - z, sets)]
        return pltpu.make_async_copy(source, into, row_sems.at[k * sets + z])

    def weight_copy(k):
        return pltpu.make_async_copy(weights[k], w_scr.at[k], w_sems.at[k])

    @pl.when(step == 0)
    def _():
        weight_copy(0).start()
        for z in range(sets):
            for k in range(len(parts)):
                row_copy(k, z).start()
        for k in range(1, len(weights)):
            weight_copy(k).start()
        for z in range(sets):
            for k in range(len(parts)):
                row_copy(k, z).wait()

    for k in range(len(weights)):

        @pl.when(step == k)
        def _():
            weight_copy(k).wait()

    w = w_scr[step].reshape(sets * depth, w_scr.shape[3])
    product[...] = jnp.dot(rows_scr[...], w, preferred_element_type=jnp.float32)
    for d2 in range(BLOCK // 8):
        low, high = [], []
        for pair in range(4):
            at = [pl.multiple_of(order_s[2 * pair + i] * BLOCK + d2 * 8, 8) for i in range(2)]
            both = swap_halves(product[pl.ds(at[0], 8), :], product[pl.ds(at[1], 8), :], 0)
            low.append(both[0])
            high.append(both[1])
        o_ref[2 * d2] = jnp.concatenate(low, axis=0).astype(jnp.bfloat16)
        o_ref[2 * d2 + 1] = jnp.concatenate(high, axis=0).astype(jnp.bfloat16)


def project(order, parts, weights):
    sets, rows, depth = parts[0].shape
    wide = weights[0].shape[2]
    n_x = 4
    groups = rows // PIECE
    return pl.pallas_call(
        project_kernel,
        out_shape=jax.ShapeDtypeStruct((groups, 8 * PIECE, n_x * wide), jnp.bfloat16),
        grid_spec=pltpu.PrefetchScalarGridSpec(
            num_scalar_prefetch=1,
            grid=(n_x,),
            in_specs=[pl.BlockSpec(memory_space=pl.ANY)] * 12,
            out_specs=pl.BlockSpec((groups, 8 * PIECE, wide), lambda k, order_s: (0, 0, order_s[8 + k])),
            scratch_shapes=[
                pltpu.VMEM((8 * rows, sets * depth), jnp.bfloat16),
                pltpu.VMEM((n_x, sets, depth, wide), jnp.bfloat16),
                pltpu.VMEM((8 * rows, wide), jnp.float32),
                pltpu.SemaphoreType.DMA((8 * sets,)),
                pltpu.SemaphoreType.DMA((n_x,)),
            ],
        ),
        compiler_params=pltpu.CompilerParams(vmem_limit_bytes=56 * MB),
        cost_estimate=pl.CostEstimate(flops=16 * rows * sets * depth * n_x * wide, bytes_accessed=18 * MB, transcendentals=0),
        name="project",
    )(order, *parts, *weights)


def arrange_kernel(i_ref, o_ref):
    n_y, _, n_c, rows, cols = i_ref.shape
    n_x = pl.num_programs(0)
    wide = cols // n_x
    for y in range(n_y):
        for x in range(n_x):
            for c in range(n_c):
                at = ((y * n_x + x) * n_c + c) * wide
                o_ref[:, at : at + wide] = i_ref[y, 0, c, :, x * wide : (x + 1) * wide]


def arrange(home):
    n_y, n_x, n_c = 4, 4, 2
    _, rows, cols = home.shape
    return pl.pallas_call(
        arrange_kernel,
        out_shape=jax.ShapeDtypeStruct((n_x * rows, n_y * n_c * cols), jnp.bfloat16),
        grid=(n_x,),
        in_specs=[pl.BlockSpec((n_y, 1, n_c, rows, cols), lambda x: (0, x, 0, 0, 0))],
        out_specs=pl.BlockSpec((rows, n_y * n_c * cols), lambda x: (x, 0)),
        compiler_params=pltpu.CompilerParams(vmem_limit_bytes=56 * MB),
        cost_estimate=pl.CostEstimate(flops=0, bytes_accessed=4 * MB, transcendentals=0),
        name="arrange",
    )(home.reshape(n_y, n_x, n_c, rows, cols))


def neighbours(axis, n, apart):
    return [(i, (i + apart) % n) for i in range(n)]


def join_kernel(*refs):
    *sources, o_ref, held, in_sems, out_sems = refs
    fetch = [pltpu.make_async_copy(source, held.at[k], in_sems.at[k]) for k, source in enumerate(sources)]
    store = [pltpu.make_async_copy(held.at[k], o_ref.at[k], out_sems.at[k]) for k in range(len(sources))]
    for copy in fetch:
        copy.start()
    for arriving, leaving in zip(fetch, store):
        arriving.wait()
        leaving.start()
    for copy in store:
        copy.wait()


def join(shards):
    n = len(shards)
    return pl.pallas_call(
        join_kernel,
        out_shape=jax.ShapeDtypeStruct((n, *shards[0].shape), shards[0].dtype),
        in_specs=[pl.BlockSpec(memory_space=pl.ANY)] * n,
        out_specs=pl.BlockSpec(memory_space=pl.ANY),
        scratch_shapes=[
            pltpu.VMEM((n, *shards[0].shape), shards[0].dtype),
            pltpu.SemaphoreType.DMA((n,)),
            pltpu.SemaphoreType.DMA((n,)),
        ],
        compiler_params=pltpu.CompilerParams(vmem_limit_bytes=56 * MB),
        cost_estimate=pl.CostEstimate(flops=0, bytes_accessed=4 * MB, transcendentals=0),
        name="join",
    )(*shards)


def ring(shard, before, after, axis):
    n = lax.axis_size(axis)
    before, after = [shard, before], [after]
    for _ in range(n // 2 - 1):
        before.append(lax.ppermute(before[-1], axis, neighbours(axis, n, 1)))
    for _ in range(n - n // 2 - 2):
        after.append(lax.ppermute(after[-1], axis, neighbours(axis, n, -1)))
    return before + after[::-1]


def hop(mine, axis, turn):
    n, n_c = lax.axis_size(axis), lax.axis_size("c")
    pairs = [(i * n_c + c, (i + turn * (1 - 2 * c)) % n * n_c + c) for i in range(n) for c in range(n_c)]
    return lax.ppermute(mine, (axis, "c"), pairs)


def on_device(queries, keys, values, out_weight, segments, send_plan):
    n_y, n_x, n_c, n_z = (lax.axis_size(a) for a in ("y", "x", "c", "z"))
    my_y, my_x, my_c = (lax.axis_index(a) for a in PLANE)
    groups = n_y * n_x * n_c
    rows, cols = queries.shape
    blocks = rows // BLOCK
    z_before, z_after = (lax.ppermute(out_weight, "z", neighbours("z", n_z, turn)) for turn in (1, -1))
    pieces = attention(queries, keys, values, segments)
    z_before, z_after, pieces = lax.optimization_barrier((z_before, z_after, pieces))
    arrived = lax.all_to_all(pieces, PLANE, 0, 0, tiled=True)
    shards, arrived = lax.optimization_barrier((ring(out_weight, z_before, z_after, "z"), arrived))
    w_own = join(shards)
    w_ahead, w_behind = hop(w_own, "x", 1), hop(w_own, "x", -1)
    slots = jnp.arange(groups * BAL)
    block_of = jnp.sum(
        jnp.where(send_plan[None, :] == slots[:, None], jnp.arange(groups * blocks)[None, :], 0), axis=1, dtype=jnp.int32
    )
    block_of = block_of.reshape(groups, BAL).T.reshape(-1)
    row_of = (block_of[:, None] * PIECE + jnp.arange(PIECE)[None, :]).reshape(-1)
    pick = (row_of[:, None] == jnp.arange(groups * blocks * PIECE)[None, :]).astype(jnp.bfloat16)
    live = jnp.dot(pick, arrived.reshape(groups * blocks * PIECE, cols), preferred_element_type=jnp.float32)
    live = live.astype(jnp.bfloat16)
    mine = lax.all_to_all(live.reshape(n_z, groups * PIECE, cols), "z", 0, 0, tiled=True)
    ahead = hop(mine, "y", 1)
    w_ahead, ahead, mine = lax.optimization_barrier((w_ahead, ahead, mine))
    w_across, behind = hop(w_ahead, "x", 1), hop(mine, "y", -1)
    parts = []
    for part in (mine, ahead, behind, hop(ahead, "y", 1)):
        parts += [part, lax.ppermute(part, "c", [(0, 1), (1, 0)])]
    from_y, from_c = jnp.divmod(jnp.arange(n_y * n_c), n_c)
    place = jnp.array([[0, 2, 6, 4], [0, 4, 6, 2]], jnp.int32)
    order = place[from_c, (my_y - from_y) % n_y] + (my_c != from_c)
    turn = 1 - 2 * my_c
    from_x = (my_x - turn * jnp.array([0, 1, -1, 2])) % n_x
    order = jnp.concatenate([order, from_x, lax.axis_index("z").reshape(1)])
    projected = project(order.astype(jnp.int32), parts, (w_own, w_ahead, w_behind, w_across))
    return arrange(lax.all_to_all(projected, PLANE, 0, 0, tiled=True))


def solution(mesh):
    fine = Mesh(mesh.devices.reshape(4, 4, 2, 8), ("y", "x", "c", "z"))
    in_specs = (P(PLANE, "z"), P(PLANE, "z"), P(PLANE, "z"), P("z", PLANE), P(PLANE), P())
    return jax.shard_map(on_device, mesh=fine, in_specs=in_specs, out_specs=P((*PLANE, "z"), None), check_vma=False)
```

```python
import functools
import math

import jax
import jax.numpy as jnp
from jax import lax
from jax.experimental import pallas as pl
from jax.experimental.pallas import tpu as pltpu
from jax.sharding import Mesh
from jax.sharding import PartitionSpec as P

HEAD = 128
TQ = 512
LONGEST = 1024
BLOCK = 128
BAL = 8
PIECE = 4
PLANE = ("y", "x", "c")
MB = 1024 * 1024


def swap_halves(even, odd, axis):
    top = lax.broadcasted_iota(jnp.int32, even.shape, axis) < PIECE
    return jnp.where(top, even, pltpu.roll(odd, PIECE, axis)), jnp.where(top, pltpu.roll(even, PIECE, axis), odd)


def attention_kernel(seg_s, q_ref, k_ref, v_ref, seg_ref, o_ref, bias_scr):
    heads = q_ref.shape[1] // HEAD
    t = pl.program_id(0)
    q0 = t * TQ
    first = seg_s[q0]
    scale = math.log2(math.e) / math.sqrt(HEAD)

    def attend(n):
        k0 = pl.multiple_of((t + 1 - n) * TQ, TQ)
        keys = k_ref[pl.ds(k0, n * TQ), :]
        values = v_ref[pl.ds(k0, n * TQ), :]
        seg_q = jnp.concatenate(
            [
                jnp.transpose(jnp.broadcast_to(seg_ref[:, pl.ds(pl.multiple_of(q0 + r, 128), 128)], (128, 128)))
                for r in range(0, TQ, 128)
            ],
            axis=0,
        )
        seg_q = jnp.concatenate([seg_q] * (TQ // 128), axis=1)
        for j in range(n):
            seg_k = seg_ref[:, pl.ds(pl.multiple_of(k0 + j * TQ, TQ), TQ)]
            allowed = seg_q == jnp.broadcast_to(seg_k, (TQ, TQ))
            if j == n - 1:
                allowed &= lax.broadcasted_iota(jnp.int32, (TQ, TQ), 1) <= lax.broadcasted_iota(jnp.int32, (TQ, TQ), 0)
            bias_scr[:, j * TQ : (j + 1) * TQ] = jnp.where(allowed, 0.0, -1e30).astype(jnp.float32)
        for h in range(heads):
            cols = slice(h * HEAD, (h + 1) * HEAD)
            scores = lax.dot_general(q_ref[:, cols], keys, (((1,), (1,)), ((), ())), preferred_element_type=jnp.float32)
            scores = scores + bias_scr[:, : n * TQ]
            top = jnp.max(scores, axis=1, keepdims=True) * scale
            weights = jnp.exp2(scores * scale - top)
            total = jnp.sum(weights, axis=1, keepdims=True)
            mixed = jnp.dot(weights.astype(jnp.bfloat16), values, preferred_element_type=jnp.float32) / total
            mixed = mixed.reshape(TQ // BLOCK, BLOCK // 8, 8, HEAD)
            runs = []
            for b in range(0, TQ // BLOCK, 2):
                low, high = swap_halves(mixed[b], mixed[b + 1], 1)
                sides = jnp.stack([low, high], axis=1).reshape(4, 4, 2, 8, HEAD)
                runs.append(sides.swapaxes(0, 1).reshape(BLOCK // PIECE, 8, HEAD))
            o_ref[:, :, cols] = jnp.concatenate(runs, axis=1).astype(jnp.bfloat16)

    @pl.when(first >= 0)
    def _():
        tiles = jnp.int32(1)
        for j in range(pl.num_programs(0) - 1):
            tiles += jnp.where((j < t) & (seg_s[j * TQ + TQ - 1] >= first), 1, 0).astype(jnp.int32)
        for n in range(1, LONGEST // TQ + 2):

            @pl.when(tiles == n)
            def _():
                attend(n)


def attention(queries, keys, values, segments):
    rows, cols = queries.shape
    heads = cols // HEAD
    groups = BLOCK // PIECE
    return pl.pallas_call(
        attention_kernel,
        out_shape=jax.ShapeDtypeStruct((groups, rows // groups, cols), jnp.bfloat16),
        grid_spec=pltpu.PrefetchScalarGridSpec(
            num_scalar_prefetch=1,
            grid=(rows // TQ,),
            in_specs=[
                pl.BlockSpec((TQ, cols), lambda t, *_: (t, 0)),
                pl.BlockSpec((rows, HEAD), lambda t, *_: (0, 0)),
                pl.BlockSpec((rows, HEAD), lambda t, *_: (0, 0)),
                pl.BlockSpec((1, rows), lambda t, *_: (0, 0)),
            ],
            out_specs=pl.BlockSpec((groups, TQ // groups, cols), lambda t, *_: (0, t, 0)),
            scratch_shapes=[pltpu.VMEM((TQ, LONGEST + TQ), jnp.float32)],
        ),
        compiler_params=pltpu.CompilerParams(vmem_limit_bytes=58 * MB),
        cost_estimate=pl.CostEstimate(flops=4 * rows * LONGEST * cols, bytes_accessed=6 * MB, transcendentals=rows * 640 * heads),
        name="attention",
    )(segments, queries, keys, values, segments.reshape(1, rows))


def project_kernel(order_s, *refs):
    parts, weights, o_ref = refs[:8], refs[8:12], refs[12]
    rows_scr, w_scr, product, row_sems, w_sems = refs[13:]
    sets, depth = w_scr.shape[1], w_scr.shape[2]
    step = pl.program_id(0)

    def row_copy(k, z):
        into = rows_scr.at[pl.ds(k * BLOCK, BLOCK), pl.ds(z * depth, depth)]
        source = parts[k].at[lax.rem(order_s[12] + sets - z, sets)]
        return pltpu.make_async_copy(source, into, row_sems.at[k * sets + z])

    def weight_copy(k):
        return pltpu.make_async_copy(weights[k], w_scr.at[k], w_sems.at[k])

    @pl.when(step == 0)
    def _():
        weight_copy(0).start()
        for z in range(sets):
            for k in range(len(parts)):
                row_copy(k, z).start()
        for k in range(1, len(weights)):
            weight_copy(k).start()
        for z in range(sets):
            for k in range(len(parts)):
                row_copy(k, z).wait()

    for k in range(len(weights)):

        @pl.when(step == k)
        def _():
            weight_copy(k).wait()

    w = w_scr[step].reshape(sets * depth, w_scr.shape[3])
    product[...] = jnp.dot(rows_scr[...], w, preferred_element_type=jnp.float32)
    for d2 in range(BLOCK // 8):
        low, high = [], []
        for pair in range(4):
            at = [pl.multiple_of(order_s[2 * pair + i] * BLOCK + d2 * 8, 8) for i in range(2)]
            both = swap_halves(product[pl.ds(at[0], 8), :], product[pl.ds(at[1], 8), :], 0)
            low.append(both[0])
            high.append(both[1])
        o_ref[2 * d2] = jnp.concatenate(low, axis=0).astype(jnp.bfloat16)
        o_ref[2 * d2 + 1] = jnp.concatenate(high, axis=0).astype(jnp.bfloat16)


def project(order, parts, weights):
    sets, rows, depth = parts[0].shape
    wide = weights[0].shape[2]
    n_x = 4
    groups = rows // PIECE
    return pl.pallas_call(
        project_kernel,
        out_shape=jax.ShapeDtypeStruct((groups, 8 * PIECE, n_x * wide), jnp.bfloat16),
        grid_spec=pltpu.PrefetchScalarGridSpec(
            num_scalar_prefetch=1,
            grid=(n_x,),
            in_specs=[pl.BlockSpec(memory_space=pl.ANY)] * 12,
            out_specs=pl.BlockSpec((groups, 8 * PIECE, wide), lambda k, order_s: (0, 0, order_s[8 + k])),
            scratch_shapes=[
                pltpu.VMEM((8 * rows, sets * depth), jnp.bfloat16),
                pltpu.VMEM((n_x, sets, depth, wide), jnp.bfloat16),
                pltpu.VMEM((8 * rows, wide), jnp.float32),
                pltpu.SemaphoreType.DMA((8 * sets,)),
                pltpu.SemaphoreType.DMA((n_x,)),
            ],
        ),
        compiler_params=pltpu.CompilerParams(vmem_limit_bytes=56 * MB),
        cost_estimate=pl.CostEstimate(flops=16 * rows * sets * depth * n_x * wide, bytes_accessed=18 * MB, transcendentals=0),
        name="project",
    )(order, *parts, *weights)


def arrange_kernel(i_ref, o_ref):
    n_y, _, n_c, rows, cols = i_ref.shape
    n_x = pl.num_programs(0)
    wide = cols // n_x
    for y in range(n_y):
        for x in range(n_x):
            for c in range(n_c):
                at = ((y * n_x + x) * n_c + c) * wide
                o_ref[:, at : at + wide] = i_ref[y, 0, c, :, x * wide : (x + 1) * wide]


def arrange(home):
    n_y, n_x, n_c = 4, 4, 2
    _, rows, cols = home.shape
    return pl.pallas_call(
        arrange_kernel,
        out_shape=jax.ShapeDtypeStruct((n_x * rows, n_y * n_c * cols), jnp.bfloat16),
        grid=(n_x, 2),
        in_specs=[pl.BlockSpec((n_y // 2, 1, n_c, rows, cols), lambda x, half: (half, x, 0, 0, 0))],
        out_specs=pl.BlockSpec((rows, n_y * n_c * cols // 2), lambda x, half: (x, half)),
        compiler_params=pltpu.CompilerParams(vmem_limit_bytes=56 * MB),
        cost_estimate=pl.CostEstimate(flops=0, bytes_accessed=4 * MB, transcendentals=0),
        name="arrange",
    )(home.reshape(n_y, n_x, n_c, rows, cols))


def neighbours(axis, n, apart):
    return [(i, (i + apart) % n) for i in range(n)]


def join_kernel(*refs):
    *sources, o_ref, held, in_sems, out_sems = refs
    fetch = [pltpu.make_async_copy(source, held.at[k], in_sems.at[k]) for k, source in enumerate(sources)]
    store = [pltpu.make_async_copy(held.at[k], o_ref.at[k], out_sems.at[k]) for k in range(len(sources))]
    for copy in fetch:
        copy.start()
    for arriving, leaving in zip(fetch, store):
        arriving.wait()
        leaving.start()
    for copy in store:
        copy.wait()


def join(shards):
    n = len(shards)
    return pl.pallas_call(
        join_kernel,
        out_shape=jax.ShapeDtypeStruct((n, *shards[0].shape), shards[0].dtype),
        in_specs=[pl.BlockSpec(memory_space=pl.ANY)] * n,
        out_specs=pl.BlockSpec(memory_space=pl.ANY),
        scratch_shapes=[
            pltpu.VMEM((n, *shards[0].shape), shards[0].dtype),
            pltpu.SemaphoreType.DMA((n,)),
            pltpu.SemaphoreType.DMA((n,)),
        ],
        compiler_params=pltpu.CompilerParams(vmem_limit_bytes=56 * MB),
        cost_estimate=pl.CostEstimate(flops=0, bytes_accessed=4 * MB, transcendentals=0),
        name="join",
    )(*shards)


def ring(shard, before, after, axis):
    n = lax.axis_size(axis)
    before, after = [shard, before], [after]
    for _ in range(n // 2 - 1):
        before.append(lax.ppermute(before[-1], axis, neighbours(axis, n, 1)))
    for _ in range(n - n // 2 - 2):
        after.append(lax.ppermute(after[-1], axis, neighbours(axis, n, -1)))
    return before + after[::-1]


def hop(mine, axis, turn):
    n, n_c = lax.axis_size(axis), lax.axis_size("c")
    pairs = [(i * n_c + c, (i + turn * (1 - 2 * c)) % n * n_c + c) for i in range(n) for c in range(n_c)]
    return lax.ppermute(mine, (axis, "c"), pairs)


def on_device(queries, keys, values, out_weight, segments, send_plan):
    n_y, n_x, n_c, n_z = (lax.axis_size(a) for a in ("y", "x", "c", "z"))
    my_y, my_x, my_c = (lax.axis_index(a) for a in PLANE)
    groups = n_y * n_x * n_c
    rows, cols = queries.shape
    blocks = rows // BLOCK
    z_before, z_after = (lax.ppermute(out_weight, "z", neighbours("z", n_z, turn)) for turn in (1, -1))
    pieces = attention(queries, keys, values, segments)
    z_before, z_after, pieces = lax.optimization_barrier((z_before, z_after, pieces))
    arrived = lax.all_to_all(pieces, PLANE, 0, 0, tiled=True)
    shards, arrived = lax.optimization_barrier((ring(out_weight, z_before, z_after, "z"), arrived))
    w_own = join(shards)
    w_ahead, w_behind = hop(w_own, "x", 1), hop(w_own, "x", -1)
    slots = jnp.arange(groups * BAL)
    block_of = jnp.sum(
        jnp.where(send_plan[None, :] == slots[:, None], jnp.arange(groups * blocks)[None, :], 0), axis=1, dtype=jnp.int32
    )
    block_of = block_of.reshape(groups, BAL).T.reshape(-1)
    row_of = (block_of[:, None] * PIECE + jnp.arange(PIECE)[None, :]).reshape(-1)
    live = jnp.take(arrived.reshape(groups * blocks * PIECE, cols), row_of, axis=0, mode="clip")
    mine = lax.all_to_all(live.reshape(n_z, groups * PIECE, cols), "z", 0, 0, tiled=True)
    ahead = hop(mine, "y", 1)
    w_ahead, ahead, mine = lax.optimization_barrier((w_ahead, ahead, mine))
    w_across, behind = hop(w_ahead, "x", 1), hop(mine, "y", -1)
    parts = []
    for part in (mine, ahead, behind, hop(ahead, "y", 1)):
        parts += [part, lax.ppermute(part, "c", [(0, 1), (1, 0)])]
    from_y, from_c = jnp.divmod(jnp.arange(n_y * n_c), n_c)
    place = jnp.array([[0, 2, 6, 4], [0, 4, 6, 2]], jnp.int32)
    order = place[from_c, (my_y - from_y) % n_y] + (my_c != from_c)
    turn = 1 - 2 * my_c
    from_x = (my_x - turn * jnp.array([0, 1, -1, 2])) % n_x
    order = jnp.concatenate([order, from_x, lax.axis_index("z").reshape(1)])
    projected = project(order.astype(jnp.int32), parts, (w_own, w_ahead, w_behind, w_across))
    return arrange(lax.all_to_all(projected, PLANE, 0, 0, tiled=True))


def solution(mesh):
    fine = Mesh(mesh.devices.reshape(4, 4, 2, 8), ("y", "x", "c", "z"))
    in_specs = (P(PLANE, "z"), P(PLANE, "z"), P(PLANE, "z"), P("z", PLANE), P(PLANE), P())
    return jax.shard_map(on_device, mesh=fine, in_specs=in_specs, out_specs=P((*PLANE, "z"), None), check_vma=False)
```
